32 devices in a mesh: seq: 8 (over z, x), chan: 2 (over core), batch: 2 (over y).
Axes of the slice: x: 2, y: 2, z: 4, core: 2. Of those that a mesh axis runs over, the one named last changes fastest.
Arguments:
- gated_input: bfloat16 [2, 1024, 4096], P('batch', 'seq', 'chan'), may hold values from -6 to 6
- query_gate: bfloat16 [2, 1024, 4096], P('batch', 'seq', 'chan'), may hold values from -1.8 to 3.8
- skip_gain: float32 [4096], P('chan'), may hold values from 0.5 to 1.5
- residues: float32 [256, 16], P('chan'), may hold values from -0.25 to 0.25
- decay_rates: float32 [256, 16], P('chan'), may hold values from 9.765625e-07 to 0.12, as said below
- cotangent: bfloat16 [2, 1024, 4096], P('batch', 'seq', 'chan'), may hold values from -200 to 200
Outputs:
- output: bfloat16 [2, 1024, 4096], P('batch', 'seq', 'chan')
- filter_update: float32 [256, 16], P('chan')
The draws below stay inside these ranges and needn't reach their ends.
Inputs may be any that keep to these rules, and one draw needn't show every extreme that they name: `decay_rates`: decay rate of each filter mode.
All inputs are finite; a program needn't handle non-finite values.
Results may differ from the reference program's by a relative error of at most 0.0052.
Values sent between devices are 32-bit elements; how exact they have to be, the bound alone decides.
A program may use at most 128 MiB of HBM per device.

```python
import jax
import jax.numpy as jnp
from jax import lax

D = 4096
MODES = 16
TOK_DEV = 128
GROUPS = 256
SEQLEN = 1024
BATCH = 2


two_pi = 6.283185307


def mode_rates(key, slow_share):
    first_key, second_key, third_key = jax.random.split(jax.random.fold_in(key, 101), 3)
    lower_log = jnp.log(jnp.float32(0.001 / SEQLEN))
    upper_log = jnp.log(jnp.float32(0.12))
    slow_log = jnp.log(jnp.float32(0.5 / SEQLEN))
    spread = jax.random.uniform(first_key, (GROUPS, MODES), jnp.float32)
    rates = jnp.exp(lower_log + (upper_log - lower_log) * spread)
    slow_rates = jnp.exp(lower_log + (slow_log - lower_log) * jax.random.uniform(second_key, (GROUPS, MODES), jnp.float32))
    chosen = jax.random.uniform(third_key, (GROUPS, MODES), jnp.float32) < slow_share
    return jnp.where(chosen, slow_rates, rates)


def sequence_wave(key):
    phase = jax.random.uniform(jax.random.fold_in(key, 202), (BATCH, 1, 1), jnp.float32, 0.0, two_pi)
    places = jnp.arange(SEQLEN, dtype=jnp.float32)[None, :, None]
    return jnp.cos(two_pi * places / 40.0 + phase)


def draw_decay_rates(key, part):
    rates = mode_rates(key, 0.0)
    return rates


def draw_residues(key, part):
    rates = mode_rates(key, 0.0)
    key = jax.random.fold_in(key, 31)
    sign_key, size_key = jax.random.split(key)
    signs = jnp.where(jax.random.uniform(sign_key, (GROUPS, MODES), jnp.float32) < 0.5, -1.0, 1.0)
    sizes = jax.random.uniform(size_key, (GROUPS, MODES), jnp.float32, 0.5, 1.5)
    floor_rate = jnp.maximum(rates, 2.0 / SEQLEN)
    return signs * sizes * 0.3 * jnp.sqrt(2.0 * floor_rate)


def draw_gated_input(key, part):
    wave = sequence_wave(key)
    key = jax.random.fold_in(key, 5)
    noise_key, width_key = jax.random.split(key)
    amplitude = jax.random.uniform(width_key, (D,), jnp.float32, 0.5, 1.5)
    noise = jnp.clip(jax.random.normal(noise_key, (BATCH, SEQLEN, D), jnp.float32), -4.0, 4.0)
    return jnp.clip(noise + 1.5 * amplitude * wave, -6.0, 6.0).astype(jnp.bfloat16)


def draw_query_gate(key, part):
    key = jax.random.fold_in(key, 7)
    noise = jnp.clip(jax.random.normal(key, (BATCH, SEQLEN, D), jnp.float32), -4.0, 4.0)
    return (1.0 + 0.7 * noise).astype(jnp.bfloat16)


def draw_cotangent(key, part):
    wave = sequence_wave(key)
    key = jax.random.fold_in(key, 23)
    keys = jax.random.split(key, 5)
    row_rise = jnp.arange(SEQLEN, dtype=jnp.float32) / SEQLEN
    col_rise = jnp.arange(D, dtype=jnp.float32) / D
    row_jitter = jax.random.uniform(keys[1], (BATCH, SEQLEN, 1), jnp.float32)
    col_jitter = jax.random.uniform(keys[2], (D,), jnp.float32)
    amplitude = jax.random.uniform(keys[4], (D,), jnp.float32, 0.5, 1.5)
    values = jnp.clip(jax.random.normal(keys[0], (BATCH, SEQLEN, D), jnp.float32), -6.0, 6.0)
    exponent = 0.5 * row_rise[None, :, None] + 0.25 * row_jitter + 0.5 * col_rise + 0.25 * col_jitter
    values = values + 1.5 * amplitude * wave
    return (values * jnp.power(10.0, exponent)).astype(jnp.bfloat16)


def steps_of(stream_key, extent, cuts, low, largest):
    def one(axis_at, blocks):
        draws = jax.random.uniform(jax.random.fold_in(jax.random.fold_in(stream_key, 6), axis_at), (blocks,), jnp.float32, low / len(cuts), largest / len(cuts))
        return jnp.repeat(jnp.exp(draws), extent[axis_at] // blocks).reshape((-1,) + (1,) * (len(extent) - axis_at - 1))

    gain = one(*cuts[0])
    for cut in cuts[1:]:
        gain = gain * one(*cut)
    return gain


def setup_inputs(seed: int = 0) -> dict:
    key_list = jax.random.split(jax.random.key(seed), 7)
    gated_input = draw_gated_input(jax.random.fold_in(key_list[6], 71), 0)
    query_gate = draw_query_gate(jax.random.fold_in(key_list[6], 71), 0)
    skip_gain = jnp.clip(0.5 + 1.0 * jax.random.uniform(key_list[2], (D,), jnp.float32) ** steps_of(key_list[2], (D,), ((0, 2),), -0.2, 0.2), 0.5, 1.5)
    residues = draw_residues(jax.random.fold_in(key_list[6], 71), 0)
    decay_rates = draw_decay_rates(jax.random.fold_in(key_list[6], 71), 0)
    cotangent = draw_cotangent(jax.random.fold_in(key_list[6], 71), 0)
    return dict(gated_input=gated_input, query_gate=query_gate, skip_gain=skip_gain, residues=residues, decay_rates=decay_rates, cotangent=cotangent)


def round_trip(values):
    return lax.optimization_barrier(values.astype(jnp.bfloat16)).astype(jnp.float32)

def lag_totals(pair_sums, steps):
    leading = pair_sums.shape[0]
    flipped = pair_sums[:, :, ::-1]
    padded = jnp.concatenate([flipped, jnp.zeros_like(flipped)], axis=2)
    flattened = padded.reshape(leading, 2 * steps * steps)[:, :steps * (2 * steps - 1)]
    skewed = flattened.reshape(leading, steps, 2 * steps - 1)
    return lax.optimization_barrier(jnp.sum(skewed, axis=1))[:, steps - 1:]

def reference(gated_input, query_gate, skip_gain, residues, decay_rates, cotangent):
    highest = lax.Precision.HIGHEST
    batch_rows, length, chans = gated_input.shape
    groups, modes = residues.shape
    group_width = chans // groups
    steps = TOK_DEV
    blocks = length // steps
    lag_index = jnp.arange(steps).astype(jnp.float32)
    powers = jnp.exp(-decay_rates[:, :, None] * lag_index)
    near_filter = round_trip(jnp.einsum('gn,gnt->gt', residues, powers, precision=highest))
    row_place = jnp.arange(steps)[:, None]
    col_place = jnp.arange(steps)[None, :]
    lag_gap = jnp.maximum(row_place - col_place, 0)
    toeplitz = jnp.where((row_place >= col_place)[None], near_filter[:, lag_gap], jnp.zeros((), jnp.float32))
    end_weight = round_trip(powers[:, :, ::-1])
    start_decay = jnp.exp(-decay_rates[:, :, None] * (lag_index + 1.0))
    start_weight = residues[:, :, None] * start_decay
    far_weight = round_trip(start_decay)
    block_decay = jnp.exp(-decay_rates * steps)
    skip_wide = skip_gain.reshape(groups, group_width)

    def advance(carry, block):
        carried, pair_total, far_total = carry
        start = (block * steps).astype(jnp.int32)
        inputs = lax.dynamic_slice_in_dim(gated_input, start, steps, 1).astype(jnp.float32).reshape(batch_rows, steps, groups, group_width)
        gates = lax.dynamic_slice_in_dim(query_gate, start, steps, 1).astype(jnp.float32).reshape(batch_rows, steps, groups, group_width)
        grads = lax.dynamic_slice_in_dim(cotangent, start, steps, 1).astype(jnp.float32).reshape(batch_rows, steps, groups, group_width)
        near_part = jnp.einsum('gts,bsgw->btgw', toeplitz, inputs, precision=highest)
        far_part = jnp.einsum('gnt,bngw->btgw', start_weight, carried, precision=highest)
        mixed = gates * (near_part + far_part + skip_wide * inputs)
        output_block = mixed.astype(jnp.bfloat16).reshape(batch_rows, steps, chans)
        conv_grad = round_trip(grads * gates)
        pair_total = pair_total + jnp.einsum('btgw,bsgw->gts', conv_grad, inputs, precision=highest)
        weighted = jnp.einsum('btgw,gnt->bgnw', conv_grad, far_weight, precision=highest)
        far_total = far_total + jnp.einsum('bgnw,bngw->gn', weighted, carried, precision=highest)
        block_state = jnp.einsum('gnt,btgw->bngw', end_weight, inputs, precision=highest)
        carried = carried * block_decay.T[None, :, :, None] + block_state
        return ((carried, pair_total, far_total), output_block)
    initial = (jnp.zeros((batch_rows, modes, groups, group_width), jnp.float32), jnp.zeros((groups, steps, steps), jnp.float32), jnp.zeros((groups, modes), jnp.float32))
    finals, outputs = lax.scan(advance, initial, jnp.arange(blocks))
    output = jnp.moveaxis(outputs, 0, 1).reshape(batch_rows, length, chans)
    lag_sums = lag_totals(finals[1], steps)
    near_grad = jnp.einsum('gt,gnt->gn', lag_sums, powers, precision=highest)
    filter_grad = near_grad + finals[2]
    grad_length = jnp.sqrt(jnp.sum(filter_grad * filter_grad) + 1e-06)
    clip_limit = jnp.sqrt(jnp.float32(groups * modes))
    return (output, filter_grad * jnp.minimum(1.0, clip_limit / grad_length))
```

```python
import functools

import jax
import jax.numpy as jnp
from jax import lax
from jax.experimental import pallas as pl
from jax.experimental.pallas import tpu as pltpu
from jax.sharding import PartitionSpec as P

MESH = pl.DeviceIdType.MESH
F32, BF16 = jnp.float32, jnp.bfloat16
HI = lax.Precision.HIGHEST
LANES = 128
CHUNKS = 2
NN = (((1,), (0,)), ((), ()))
NT = (((1,), (1,)), ((), ()))
TN = (((0,), (0,)), ((), ()))


def dot(a, b, dims=NN, precision=None):
    return lax.dot_general(a, b, dims, precision=precision, preferred_element_type=F32)


def iota(shape, dim):
    return lax.broadcasted_iota(jnp.int32, shape, dim)


def split(a):
    high = a.astype(BF16)
    return high, (a - high.astype(F32)).astype(BF16)


def kernel(
    sizes, rounds, width, modes,
    x_ref, q_ref, ct_ref, skip_ref, res_ref, rate_ref,
    out_ref, upd_ref,
    s_ref, from_mate, dec_ref, filt_ref, q_sum, even_part, chain_in, chain_out,
    own_c, mate_c, other_c, near_ref, grad_in, sd_ref, fall_ref, g_ref, r1, tot_ref, later,
    mate_sem, chain_sem, back_sem, r1_send, r1_recv, later_send, later_recv,
):
    n_seq, n_batch, n_chan = sizes
    pairs = n_seq // 2
    steps, chans = x_ref.shape
    tiles = chans // LANES
    half = tiles // 2
    per = LANES // width
    lane_of = iota((1, LANES), 1)
    seq, bat, cha = (lax.axis_index(a) for a in ("seq", "batch", "chan"))
    parity, line = lax.rem(seq, 2), lax.div(seq, 2)

    def dev(s, b=bat, c=cha):
        return {"seq": s, "batch": b, "chan": c}

    mate = dev(seq + 1 - 2 * parity)
    group_row = iota((LANES, LANES), 0) // width
    group_col = iota((LANES, LANES), 1) // width
    same = group_row == group_col
    lower = iota((steps, steps), 0) >= iota((steps, steps), 1)
    index_sum = iota((steps, steps), 0) + iota((steps, steps), 1)
    corner = index_sum <= steps - 1
    reverse = jnp.where(index_sum == steps - 1, 1.0, 0.0).astype(BF16)
    pick = (iota((per, LANES), 0) == iota((per, LANES), 1) // modes)

    first = [(m & 1, (m >> 1) & 1, (m >> 2) & 1) for m in range(1, 8)]

    def flip(v, bit):
        return 1 - v if bit else v

    first = [(flip(parity, dp), flip(bat, db), flip(cha, dc)) for dp, db, dc in first]
    barrier = pltpu.get_barrier_semaphore()

    def greet(d):
        pl.semaphore_signal(barrier, inc=1, device_id=d, device_id_type=MESH)

    for p, b, c in first:
        greet(dev(2 * line + p, b, c))
    count = len(first)
    hops = []
    for stride, radix in rounds:
        digit = lax.rem(lax.div(line, stride), radix)
        peers = []
        for o in range(1, radix):
            there = lax.rem(digit + o, radix)
            peers.append((there, dev(2 * (line + (there - digit) * stride) + parity)))
        hops.append((digit, peers))
        for _, d in peers:
            greet(d)
        count += radix - 1

    @pl.when(line > 0)
    def _():
        greet(dev(seq - 2))

    @pl.when(line < pairs - 1)
    def _():
        greet(dev(seq + 2))

    count = count + jnp.where(line > 0, 1, 0) + jnp.where(line < pairs - 1, 1, 0)

    back = (steps - 1 - iota((steps, LANES), 0)).astype(F32)
    select = (iota((modes, LANES), 1) % modes) == iota((modes, LANES), 0)
    one_hot = jnp.where(same, 1.0, 0.0).astype(F32)

    def state_tile(h, j):
        i = h * half + j
        at = pl.ds(pl.multiple_of(i * LANES, LANES), LANES)
        lanes = pl.ds(pl.multiple_of(j * LANES, LANES), LANES)
        rate = rate_ref[pl.ds(i, 1), :]
        res = res_ref[pl.ds(i, 1), :]
        falling = jnp.exp(-rate * back)
        fall_ref[i] = falling
        full = dot(falling.astype(BF16), x_ref[:, at], TN)
        full = jnp.where(same, full, 0.0).reshape(per, modes, LANES)
        s_ref[h, :, lanes] = jnp.sum(full, axis=0)
        weight = jnp.where(pick, res, 0.0)
        filt_ref[pl.ds(pl.multiple_of(i * per, per), per), :] = dot(weight, falling, NT, HI)
        decay = jnp.exp(-rate * float(steps))
        dec_ref[h, :, lanes] = dot(jnp.where(select, decay, 0.0), one_hot, NN, HI)

    other = 1 - parity

    def other_tile(j, _):
        state_tile(other, j)
        return 0

    def own_tile(j, _):
        state_tile(parity, j)
        return 0

    lax.fori_loop(0, half, other_tile, 0)
    pl.semaphore_wait(barrier, count)
    to_mate = pltpu.make_async_remote_copy(
        s_ref.at[other], from_mate, mate_sem.at[0], mate_sem.at[1], device_id=mate,
        device_id_type=MESH,
    )
    to_mate.start()
    lax.fori_loop(0, half, own_tile, 0)

    part = half * LANES // CHUNKS

    def chain_copy(k):
        return pltpu.make_async_remote_copy(
            chain_out.at[k], chain_in.at[k], chain_sem.at[0, k], chain_sem.at[1, k],
            device_id=dev(jnp.minimum(seq + 2, n_seq - 1 - (1 - parity))), device_id_type=MESH,
        )

    def back_copy(k):
        return pltpu.make_async_remote_copy(
            mate_c.at[k], other_c.at[k], back_sem.at[0, k], back_sem.at[1, k], device_id=mate,
            device_id_type=MESH,
        )

    def chain_step():
        to_mate.wait_recv()
        for k in range(CHUNKS):
            cols = slice(k * part, (k + 1) * part)
            mine, his = s_ref[parity, :, cols], from_mate[:, cols]
            early = jnp.where(parity == 0, mine, his)
            late = jnp.where(parity == 0, his, mine)
            q_sum[:, cols] = dec_ref[parity, :, cols] * early + late
            even_part[:, cols] = early

        for k in range(CHUNKS):
            cols = slice(k * part, (k + 1) * part)
            decay = dec_ref[parity, :, cols]
            early = even_part[:, cols]

            def finish(carry):
                @pl.when(line < pairs - 1)
                def _():
                    chain_out[k] = decay * decay * carry + q_sum[:, cols]
                    chain_copy(k).start()

                after = decay * carry + early
                mate_c[k] = jnp.where(parity == 0, after, carry)
                back_copy(k).start()
                own_c[k] = jnp.where(parity == 0, carry, after)

            @pl.when(line == 0)
            def _():
                finish(jnp.zeros((modes, part), F32))

            @pl.when(line > 0)
            def _():
                chain_copy(k).wait_recv()
                finish(chain_in[k])

    trigger = jnp.minimum(2 + lax.div(line * tiles, pairs), tiles - 1)
    ahead = (iota((steps, LANES), 0) + 1).astype(F32)

    def near_tile(i, _):
        @pl.when(i == trigger)
        def _():
            chain_step()

        at = pl.ds(pl.multiple_of(i * LANES, LANES), LANES)
        x = x_ref[:, at]
        grad = (ct_ref[:, at].astype(F32) * q_ref[:, at].astype(F32)).astype(BF16)
        grad_in[:, at] = grad
        zero = jnp.zeros((), BF16)
        stacked = jnp.concatenate(
            [jnp.where(lane_of // width == g, x, zero) for g in range(per)], axis=0
        )
        filt = filt_ref[pl.ds(pl.multiple_of(i * per, per), per), :]
        filt = filt.astype(BF16).astype(F32)
        blocks = []
        for g in range(per):
            rows = jnp.broadcast_to(filt[g : g + 1, :], (steps, steps))
            rows = pltpu.roll(rows, 1, 1, stride=1, stride_axis=0)
            blocks.append(jnp.where(lower, rows, 0.0).astype(BF16))
        near = dot(jnp.concatenate(blocks, axis=1), stacked)
        near_ref[:, at] = near + skip_ref[:, at] * x.astype(F32)
        turned = dot(reverse, grad).astype(BF16)
        pair_sums = dot(stacked, turned, NT)
        totals = []
        for g in range(per):
            block = jnp.where(corner, pair_sums[g * steps : (g + 1) * steps], 0.0)
            block = pltpu.roll(block, 0, 1, stride=1, stride_axis=0)
            totals.append(jnp.sum(block, axis=0, keepdims=True))
        lag_sums = jnp.concatenate(totals, axis=0)
        rate = rate_ref[pl.ds(i, 1), :]
        start = jnp.exp(-rate * ahead)
        sd_ref[i] = start
        wide = dot(lag_sums, jnp.where(pick, 1.0, 0.0), TN, HI)
        g_ref[pl.ds(i, 1), :] = jnp.sum(wide * fall_ref[i], axis=0, keepdims=True)
        return 0

    lax.fori_loop(0, tiles, near_tile, 0)

    per_chunk = half // CHUNKS

    def far_tile(h, k, j, carried_ref):
        i = h * half + k * per_chunk + j
        at = pl.ds(pl.multiple_of(i * LANES, LANES), LANES)
        lanes = pl.ds(pl.multiple_of(j * LANES, LANES), LANES)
        carried = carried_ref[k, :, lanes]
        carried = jnp.broadcast_to(carried[None], (per, modes, LANES)).reshape(LANES, LANES)
        c_hi, c_lo = split(jnp.where(same, carried, 0.0))
        start = sd_ref[i]
        a_hi, a_lo = split(res_ref[pl.ds(i, 1), :] * start)
        far = dot(
            jnp.concatenate([a_hi, a_hi, a_lo], axis=1),
            jnp.concatenate([c_hi, c_lo, c_hi], axis=0),
        )
        gate = q_ref[:, at].astype(F32)
        out_ref[:, at] = (gate * (near_ref[:, at] + far)).astype(BF16)
        grad = grad_in[:, at]
        mixed = dot(grad, c_hi, NT) + dot(grad, c_lo, NT)
        gain = jnp.sum(mixed * start.astype(BF16).astype(F32), axis=0, keepdims=True)
        g_ref[pl.ds(i, 1), :] += gain

    def far_loop(h, k, carried_ref):
        def body(j, _):
            far_tile(h, k, j, carried_ref)
            return 0

        lax.fori_loop(0, per_chunk, body, 0)

    for k in range(CHUNKS):
        far_loop(parity, k, own_c)
    for k in range(CHUNKS):
        back_copy(k).wait_recv()
        far_loop(other, k, other_c)

    my_slot = cha * 4 + bat * 2 + parity
    r1[my_slot] = g_ref[...]
    sends = []
    for m, (p, b, c) in enumerate(first):
        copy = pltpu.make_async_remote_copy(
            g_ref, r1.at[my_slot], r1_send.at[m], r1_recv.at[my_slot],
            device_id=dev(2 * line + p, b, c), device_id_type=MESH,
        )
        copy.start()
        sends.append(copy)
    for m, (p, b, c) in enumerate(first):
        slot = c * 4 + b * 2 + p
        pltpu.make_async_remote_copy(
            g_ref, r1.at[slot], r1_send.at[m], r1_recv.at[slot],
            device_id=dev(2 * line + p, b, c), device_id_type=MESH,
        ).wait_recv()
    tot_ref[0, 0] = (r1[0] + r1[1]) + (r1[2] + r1[3])
    tot_ref[0, 1] = (r1[4] + r1[5]) + (r1[6] + r1[7])
    base = 0
    for r, ((stride, radix), (digit, peers)) in enumerate(zip(rounds, hops)):
        here = base + digit
        later[here] = tot_ref[r]
        for o, (there, d) in enumerate(peers):
            copy = pltpu.make_async_remote_copy(
                tot_ref.at[r], later.at[here], later_send.at[base + o], later_recv.at[here],
                device_id=d, device_id_type=MESH,
            )
            copy.start()
            sends.append(copy)
        for o, (there, d) in enumerate(peers):
            pltpu.make_async_remote_copy(
                tot_ref.at[r], later.at[base + there], later_send.at[base + o],
                later_recv.at[base + there], device_id=d, device_id_type=MESH,
            ).wait_recv()
        total = later[base]
        for o in range(1, radix):
            total = total + later[base + o]
        tot_ref[r + 1] = total
        base += radix
    done = len(rounds)
    square = jnp.sum(tot_ref[done] * tot_ref[done], keepdims=True).reshape(1, 1)
    limit = jnp.sqrt(jnp.float32(tiles * LANES * n_chan))
    scale = jnp.minimum(1.0, limit / jnp.sqrt(square + 1e-06))
    upd_ref[...] = tot_ref[done, cha] * scale

    for copy in sends:
        copy.wait_send()
    to_mate.wait_send()
    for k in range(CHUNKS):
        back_copy(k).wait_send()

        @pl.when(line < pairs - 1)
        def _():
            chain_copy(k).wait_send()


def on_device(sizes, gated_input, query_gate, skip_gain, residues, decay_rates, cotangent):
    _, steps, chans = gated_input.shape
    groups, modes = residues.shape
    width = chans // groups
    tiles = chans // LANES
    half = tiles // 2
    pairs = sizes[0] // 2
    rounds, stride = [], 1
    while stride < pairs:
        radix = 4 if (pairs // stride) % 4 == 0 else 2
        rounds.append((stride, radix))
        stride *= radix
    slots = max(1, sum(r for _, r in rounds))
    part = half * LANES // CHUNKS
    wide = half * LANES
    vmem = pl.BlockSpec(memory_space=pltpu.VMEM)
    dma = pltpu.SemaphoreType.DMA
    output, update = pl.pallas_call(
        functools.partial(kernel, sizes, rounds, width, modes),
        out_shape=(
            jax.ShapeDtypeStruct((steps, chans), BF16),
            jax.ShapeDtypeStruct((tiles, LANES), F32),
        ),
        in_specs=[vmem] * 6,
        out_specs=(vmem, vmem),
        scratch_shapes=[
            pltpu.VMEM((2, modes, wide), F32),
            pltpu.VMEM((modes, wide), F32),
            pltpu.VMEM((2, modes, wide), F32),
            pltpu.VMEM((groups, steps), F32),
            pltpu.VMEM((modes, wide), F32),
            pltpu.VMEM((modes, wide), F32),
            pltpu.VMEM((CHUNKS, modes, part), F32),
            pltpu.VMEM((CHUNKS, modes, part), F32),
            pltpu.VMEM((CHUNKS, modes, part), F32),
            pltpu.VMEM((CHUNKS, modes, part), F32),
            pltpu.VMEM((CHUNKS, modes, part), F32),
            pltpu.VMEM((steps, chans), F32),
            pltpu.VMEM((steps, chans), BF16),
            pltpu.VMEM((tiles, steps, LANES), F32),
            pltpu.VMEM((tiles, steps, LANES), F32),
            pltpu.VMEM((tiles, LANES), F32),
            pltpu.VMEM((8, tiles, LANES), F32),
            pltpu.VMEM((len(rounds) + 1, 2, tiles, LANES), F32),
            pltpu.VMEM((slots, 2, tiles, LANES), F32),
            dma((2,)),
            dma((2, CHUNKS)),
            dma((2, CHUNKS)),
            dma((7,)),
            dma((8,)),
            dma((slots,)),
            dma((slots,)),
        ],
        compiler_params=pltpu.CompilerParams(
            collective_id=0, has_side_effects=True, vmem_limit_bytes=48 * 1024 * 1024
        ),
    )(
        gated_input.reshape(steps, chans),
        query_gate.reshape(steps, chans),
        cotangent.reshape(steps, chans),
        skip_gain.reshape(1, chans),
        residues.reshape(tiles, LANES),
        decay_rates.reshape(tiles, LANES),
    )
    return output.reshape(gated_input.shape), update.reshape(groups, modes)


def solution(mesh):
    sizes = tuple(mesh.shape[a] for a in ("seq", "batch", "chan"))
    return jax.shard_map(
        functools.partial(on_device, sizes),
        mesh=mesh,
        in_specs=(
            P("batch", "seq", "chan"),
            P("batch", "seq", "chan"),
            P("chan"),
            P("chan", None),
            P("chan", None),
            P("batch", "seq", "chan"),
        ),
        out_specs=(P("batch", "seq", "chan"), P("chan", None)),
        check_vma=False,
    )
```

```python
import functools

import jax
import jax.numpy as jnp
from jax import lax
from jax.experimental import pallas as pl
from jax.experimental.pallas import tpu as pltpu
from jax.sharding import PartitionSpec as P

MESH = pl.DeviceIdType.MESH
F32, BF16 = jnp.float32, jnp.bfloat16
HI = lax.Precision.HIGHEST
LANES = 128
CHUNKS = 2
NN = (((1,), (0,)), ((), ()))
NT = (((1,), (1,)), ((), ()))
TN = (((0,), (0,)), ((), ()))


def dot(a, b, dims=NN, precision=None):
    return lax.dot_general(a, b, dims, precision=precision, preferred_element_type=F32)


def iota(shape, dim):
    return lax.broadcasted_iota(jnp.int32, shape, dim)


def split(a):
    high = a.astype(BF16)
    return high, (a - high.astype(F32)).astype(BF16)


def split3(a):
    high, rest = a.astype(BF16), a
    rest = a - high.astype(F32)
    mid = rest.astype(BF16)
    return high, mid, (rest - mid.astype(F32)).astype(BF16)


def rows_by_one_hot(parts, one_hot):
    stacked = jnp.concatenate([p.astype(F32) for p in parts], axis=0).astype(BF16)
    return stacked, jnp.concatenate([one_hot] * len(parts), axis=0)


def kernel(
    sizes, rounds, width, modes,
    x_hbm, q_hbm, ct_hbm, skip_hbm, res_hbm, rate_hbm,
    out_ref, upd_ref,
    x_ref, q_ref, ct_ref, skip_ref, res_in, rate_in, res_ref, rate_ref, in_sem,
    s_ref, from_mate, dec_ref, filt_ref, q_sum, even_part, chain_in, chain_out,
    own_c, mate_c, other_c, near_ref, grad_in, sd_ref, fall_ref, g_ref, r1, tot_ref, later,
    mate_sem, chain_sem, back_sem, r1_send, r1_recv, later_send, later_recv,
):
    n_seq, n_batch, n_chan = sizes
    pairs = n_seq // 2
    steps, chans = x_hbm.shape
    tiles = chans // LANES
    half = tiles // 2
    per = LANES // width
    lane_of = iota((1, LANES), 1)
    seq, bat, cha = (lax.axis_index(a) for a in ("seq", "batch", "chan"))
    parity, line = lax.rem(seq, 2), lax.div(seq, 2)

    def dev(s, b=bat, c=cha):
        return {"seq": s, "batch": b, "chan": c}

    def fetch(n, src, dst):
        copy = pltpu.make_async_copy(src, dst, in_sem.at[n])
        copy.start()
        return copy

    def columns(h):
        return pl.ds(pl.multiple_of(h * (half * LANES), LANES), half * LANES)

    other = 1 - parity
    get_rate = fetch(0, rate_hbm, rate_in)
    get_res = fetch(1, res_hbm, res_in)
    get_x1 = fetch(2, x_hbm.at[:, columns(other)], x_ref.at[:, columns(other)])
    get_x2 = fetch(3, x_hbm.at[:, columns(parity)], x_ref.at[:, columns(parity)])
    get_q = fetch(4, q_hbm, q_ref)
    get_ct = fetch(5, ct_hbm, ct_ref)
    get_skip = fetch(6, skip_hbm, skip_ref)

    mate = dev(seq + 1 - 2 * parity)
    group_row = iota((LANES, LANES), 0) // width
    group_col = iota((LANES, LANES), 1) // width
    same = group_row == group_col
    lower = iota((steps, steps), 0) >= iota((steps, steps), 1)
    index_sum = iota((steps, steps), 0) + iota((steps, steps), 1)
    corner = index_sum <= steps - 1
    reverse = jnp.where(index_sum == steps - 1, 1.0, 0.0).astype(BF16)
    pick = (iota((per, LANES), 0) == iota((per, LANES), 1) // modes)

    first = [(m & 1, (m >> 1) & 1, (m >> 2) & 1) for m in range(1, 8)]

    def flip(v, bit):
        return 1 - v if bit else v

    first = [(flip(parity, dp), flip(bat, db), flip(cha, dc)) for dp, db, dc in first]
    barrier = pltpu.get_barrier_semaphore()

    def greet(d):
        pl.semaphore_signal(barrier, inc=1, device_id=d, device_id_type=MESH)

    for p, b, c in first:
        greet(dev(2 * line + p, b, c))
    count = len(first)
    hops = []
    for stride, radix in rounds:
        digit = lax.rem(lax.div(line, stride), radix)
        peers = []
        for o in range(1, radix):
            there = lax.rem(digit + o, radix)
            peers.append((there, dev(2 * (line + (there - digit) * stride) + parity)))
        hops.append((digit, peers))
        for _, d in peers:
            greet(d)
        count += radix - 1

    @pl.when(line > 0)
    def _():
        greet(dev(seq - 2))

    @pl.when(line < pairs - 1)
    def _():
        greet(dev(seq + 2))

    count = count + jnp.where(line > 0, 1, 0) + jnp.where(line < pairs - 1, 1, 0)

    back = (steps - 1 - iota((steps, LANES), 0)).astype(F32)
    select = (iota((modes, LANES), 1) % modes) == iota((modes, LANES), 0)
    one_hot = jnp.where(same, 1.0, 0.0).astype(BF16)

    def state_tile(h, j):
        i = h * half + j
        at = pl.ds(pl.multiple_of(i * LANES, LANES), LANES)
        lanes = pl.ds(pl.multiple_of(j * LANES, LANES), LANES)
        rate = rate_ref[pl.ds(i, 1), :]
        res = res_ref[pl.ds(i, 1), :]
        falling = jnp.exp(-rate * back)
        fall_ref[i] = falling
        f_hi, f_lo = split(falling)
        full = dot(f_hi, x_ref[:, at], TN)
        full = jnp.where(same, full, 0.0).reshape(per, modes, LANES)
        s_ref[h, :, lanes] = jnp.sum(full, axis=0)
        w_hi, w_lo = split(jnp.where(pick, res, 0.0))
        filt_ref[pl.ds(pl.multiple_of(i * per, per), per), :] = dot(
            jnp.concatenate([w_hi, w_hi, w_lo], axis=1),
            jnp.concatenate([f_hi, f_lo, f_hi], axis=1),
            NT,
        )
        decay = jnp.exp(-rate * float(steps))
        spread = dot(
            jnp.concatenate(split3(jnp.where(select, decay, 0.0)), axis=0), one_hot
        )
        dec_ref[h, :, lanes] = spread[:modes] + spread[modes : 2 * modes] + spread[2 * modes :]

    def other_two(j, _):
        state_tile(other, 2 * j)
        state_tile(other, 2 * j + 1)
        return 0

    def own_two(j, _):
        state_tile(parity, 2 * j)
        state_tile(parity, 2 * j + 1)
        return 0

    groups = tiles * per
    row_group = lax.rem(iota((groups, LANES), 0), per) == iota((groups, LANES), 1) // modes
    mode_hot = jnp.where(select, 1.0, 0.0).astype(BF16)

    def by_rows(ref):
        left, right = rows_by_one_hot(split3(ref[...]), mode_hot)
        wide = jnp.where(row_group, dot(left, right, TN), 0.0)
        return jnp.sum(wide.reshape(tiles, per, LANES), axis=1)

    get_rate.wait()
    rate_ref[...] = by_rows(rate_in)
    get_res.wait()
    res_ref[...] = by_rows(res_in)
    get_x1.wait()
    lax.fori_loop(0, half // 2, other_two, 0)
    pl.semaphore_wait(barrier, count)
    to_mate = pltpu.make_async_remote_copy(
        s_ref.at[other], from_mate, mate_sem.at[0], mate_sem.at[1], device_id=mate,
        device_id_type=MESH,
    )
    to_mate.start()
    get_x2.wait()
    lax.fori_loop(0, half // 2, own_two, 0)
    get_q.wait()
    get_ct.wait()
    get_skip.wait()

    part = half * LANES // CHUNKS

    def chain_copy(k):
        return pltpu.make_async_remote_copy(
            chain_out.at[k], chain_in.at[k], chain_sem.at[0, k], chain_sem.at[1, k],
            device_id=dev(jnp.minimum(seq + 2, n_seq - 1 - (1 - parity))), device_id_type=MESH,
        )

    def back_copy(k):
        return pltpu.make_async_remote_copy(
            mate_c.at[k], other_c.at[k], back_sem.at[0, k], back_sem.at[1, k], device_id=mate,
            device_id_type=MESH,
        )

    def chain_step():
        to_mate.wait_recv()
        for k in range(CHUNKS):
            cols = slice(k * part, (k + 1) * part)
            mine, his = s_ref[parity, :, cols], from_mate[:, cols]
            early = jnp.where(parity == 0, mine, his)
            late = jnp.where(parity == 0, his, mine)
            q_sum[:, cols] = dec_ref[parity, :, cols] * early + late
            even_part[:, cols] = early

        for k in range(CHUNKS):
            cols = slice(k * part, (k + 1) * part)
            decay = dec_ref[parity, :, cols]
            early = even_part[:, cols]

            def finish(carry):
                @pl.when(line < pairs - 1)
                def _():
                    chain_out[k] = decay * decay * carry + q_sum[:, cols]
                    chain_copy(k).start()

                after = decay * carry + early
                mate_c[k] = jnp.where(parity == 0, after, carry)
                back_copy(k).start()
                own_c[k] = jnp.where(parity == 0, carry, after)

            @pl.when(line == 0)
            def _():
                finish(jnp.zeros((modes, part), F32))

            @pl.when(line > 0)
            def _():
                chain_copy(k).wait_recv()
                finish(chain_in[k])

    trigger = jnp.minimum(1 + lax.div(line * half, pairs), half - 1)
    ahead = (iota((steps, LANES), 0) + 1).astype(F32)

    def near_tile(i):
        at = pl.ds(pl.multiple_of(i * LANES, LANES), LANES)
        x = x_ref[:, at]
        grad = (ct_ref[:, at].astype(F32) * q_ref[:, at].astype(F32)).astype(BF16)
        grad_in[:, at] = grad
        zero = jnp.zeros((), BF16)
        stacked = jnp.concatenate(
            [jnp.where(lane_of // width == g, x, zero) for g in range(per)], axis=0
        )
        filt = filt_ref[pl.ds(pl.multiple_of(i * per, per), per), :]
        filt = filt.astype(BF16).astype(F32)
        blocks = []
        for g in range(per):
            rows = jnp.broadcast_to(filt[g : g + 1, :], (steps, steps))
            rows = pltpu.roll(rows, 1, 1, stride=1, stride_axis=0)
            blocks.append(jnp.where(lower, rows, 0.0).astype(BF16))
        near = dot(jnp.concatenate(blocks, axis=1), stacked)
        near_ref[:, at] = near + skip_ref[:, at] * x.astype(F32)
        turned = dot(reverse, grad).astype(BF16)
        pair_sums = dot(stacked, turned, NT)
        totals = []
        for g in range(per):
            block = jnp.where(corner, pair_sums[g * steps : (g + 1) * steps], 0.0)
            block = pltpu.roll(block, 0, 1, stride=1, stride_axis=0)
            totals.append(jnp.sum(block, axis=0, keepdims=True))
        lag_sums = jnp.concatenate(totals, axis=0)
        rate = rate_ref[pl.ds(i, 1), :]
        start = jnp.exp(-rate * ahead)
        sd_ref[i] = start
        left, right = rows_by_one_hot(split3(lag_sums), jnp.where(pick, 1.0, 0.0))
        wide = dot(left, right.astype(BF16), TN)
        g_ref[pl.ds(i, 1), :] = jnp.sum(wide * fall_ref[i], axis=0, keepdims=True)

    def near_two(i, _):
        @pl.when(i == trigger)
        def _():
            chain_step()

        near_tile(2 * i)
        near_tile(2 * i + 1)
        return 0

    lax.fori_loop(0, half, near_two, 0)

    per_chunk = half // CHUNKS

    def far_tile(h, k, j, carried_ref):
        i = h * half + k * per_chunk + j
        at = pl.ds(pl.multiple_of(i * LANES, LANES), LANES)
        lanes = pl.ds(pl.multiple_of(j * LANES, LANES), LANES)
        carried = carried_ref[k, :, lanes]
        carried = jnp.broadcast_to(carried[None], (per, modes, LANES)).reshape(LANES, LANES)
        c_hi, c_lo = split(jnp.where(same, carried, 0.0))
        start = sd_ref[i]
        a_hi, a_lo = split(res_ref[pl.ds(i, 1), :] * start)
        far = dot(
            jnp.concatenate([a_hi, a_hi, a_lo], axis=1),
            jnp.concatenate([c_hi, c_lo, c_hi], axis=0),
        )
        gate = q_ref[:, at].astype(F32)
        out_ref[:, at] = (gate * (near_ref[:, at] + far)).astype(BF16)
        grad = grad_in[:, at]
        mixed = dot(grad, c_hi, NT) + dot(grad, c_lo, NT)
        gain = jnp.sum(mixed * start.astype(BF16).astype(F32), axis=0, keepdims=True)
        g_ref[pl.ds(i, 1), :] += gain

    def far_loop(h, k, carried_ref):
        def body(j, _):
            far_tile(h, k, 2 * j, carried_ref)
            far_tile(h, k, 2 * j + 1, carried_ref)
            return 0

        lax.fori_loop(0, per_chunk // 2, body, 0)

    for k in range(CHUNKS):
        far_loop(parity, k, own_c)
    for k in range(CHUNKS):
        back_copy(k).wait_recv()
        far_loop(other, k, other_c)

    my_slot = cha * 4 + bat * 2 + parity
    r1[my_slot] = g_ref[...]
    sends = []
    for m, (p, b, c) in enumerate(first):
        copy = pltpu.make_async_remote_copy(
            g_ref, r1.at[my_slot], r1_send.at[m], r1_recv.at[my_slot],
            device_id=dev(2 * line + p, b, c), device_id_type=MESH,
        )
        copy.start()
        sends.append(copy)
    for m, (p, b, c) in enumerate(first):
        slot = c * 4 + b * 2 + p
        pltpu.make_async_remote_copy(
            g_ref, r1.at[slot], r1_send.at[m], r1_recv.at[slot],
            device_id=dev(2 * line + p, b, c), device_id_type=MESH,
        ).wait_recv()
    tot_ref[0, 0] = (r1[0] + r1[1]) + (r1[2] + r1[3])
    tot_ref[0, 1] = (r1[4] + r1[5]) + (r1[6] + r1[7])
    base = 0
    for r, ((stride, radix), (digit, peers)) in enumerate(zip(rounds, hops)):
        here = base + digit
        later[here] = tot_ref[r]
        for o, (there, d) in enumerate(peers):
            copy = pltpu.make_async_remote_copy(
                tot_ref.at[r], later.at[here], later_send.at[base + o], later_recv.at[here],
                device_id=d, device_id_type=MESH,
            )
            copy.start()
            sends.append(copy)
        for o, (there, d) in enumerate(peers):
            pltpu.make_async_remote_copy(
                tot_ref.at[r], later.at[base + there], later_send.at[base + o],
                later_recv.at[base + there], device_id=d, device_id_type=MESH,
            ).wait_recv()
        total = later[base]
        for o in range(1, radix):
            total = total + later[base + o]
        tot_ref[r + 1] = total
        base += radix
    done = len(rounds)
    square = jnp.sum(tot_ref[done] * tot_ref[done], keepdims=True).reshape(1, 1)
    limit = jnp.sqrt(jnp.float32(tiles * LANES * n_chan))
    scale = jnp.minimum(1.0, limit / jnp.sqrt(square + 1e-06))
    rows = tot_ref[done, cha] * scale
    rows = jnp.broadcast_to(rows[:, None, :], (tiles, per, LANES)).reshape(groups, LANES)
    rows = jnp.concatenate(split3(jnp.where(row_group, rows, 0.0)), axis=1)
    upd_ref[...] = dot(jnp.concatenate([mode_hot] * 3, axis=1), rows, NT)

    for copy in sends:
        copy.wait_send()
    to_mate.wait_send()
    for k in range(CHUNKS):
        back_copy(k).wait_send()

        @pl.when(line < pairs - 1)
        def _():
            chain_copy(k).wait_send()


def on_device(sizes, gated_input, query_gate, skip_gain, residues, decay_rates, cotangent):
    _, steps, chans = gated_input.shape
    groups, modes = residues.shape
    width = chans // groups
    tiles = chans // LANES
    half = tiles // 2
    pairs = sizes[0] // 2
    rounds, stride = [], 1
    while stride < pairs:
        radix = 4 if (pairs // stride) % 4 == 0 else 2
        rounds.append((stride, radix))
        stride *= radix
    slots = max(1, sum(r for _, r in rounds))
    part = half * LANES // CHUNKS
    wide = half * LANES
    vmem = pl.BlockSpec(memory_space=pltpu.VMEM)
    dma = pltpu.SemaphoreType.DMA
    output, update = pl.pallas_call(
        functools.partial(kernel, sizes, rounds, width, modes),
        out_shape=(
            jax.ShapeDtypeStruct((steps, chans), BF16),
            jax.ShapeDtypeStruct((modes, groups), F32),
        ),
        in_specs=[pl.BlockSpec(memory_space=pltpu.HBM)] * 6,
        out_specs=(vmem, vmem),
        scratch_shapes=[
            pltpu.VMEM((steps, chans), BF16),
            pltpu.VMEM((steps, chans), BF16),
            pltpu.VMEM((steps, chans), BF16),
            pltpu.VMEM((1, chans), F32),
            pltpu.VMEM((modes, groups), F32),
            pltpu.VMEM((modes, groups), F32),
            pltpu.VMEM((tiles, LANES), F32),
            pltpu.VMEM((tiles, LANES), F32),
            dma((7,)),
            pltpu.VMEM((2, modes, wide), F32),
            pltpu.VMEM((modes, wide), F32),
            pltpu.VMEM((2, modes, wide), F32),
            pltpu.VMEM((groups, steps), F32),
            pltpu.VMEM((modes, wide), F32),
            pltpu.VMEM((modes, wide), F32),
            pltpu.VMEM((CHUNKS, modes, part), F32),
            pltpu.VMEM((CHUNKS, modes, part), F32),
            pltpu.VMEM((CHUNKS, modes, part), F32),
            pltpu.VMEM((CHUNKS, modes, part), F32),
            pltpu.VMEM((CHUNKS, modes, part), F32),
            pltpu.VMEM((steps, chans), F32),
            pltpu.VMEM((steps, chans), BF16),
            pltpu.VMEM((tiles, steps, LANES), F32),
            pltpu.VMEM((tiles, steps, LANES), F32),
            pltpu.VMEM((tiles, LANES), F32),
            pltpu.VMEM((8, tiles, LANES), F32),
            pltpu.VMEM((len(rounds) + 1, 2, tiles, LANES), F32),
            pltpu.VMEM((slots, 2, tiles, LANES), F32),
            dma((2,)),
            dma((2, CHUNKS)),
            dma((2, CHUNKS)),
            dma((7,)),
            dma((8,)),
            dma((slots,)),
            dma((slots,)),
        ],
        compiler_params=pltpu.CompilerParams(
            collective_id=0, has_side_effects=True, vmem_limit_bytes=48 * 1024 * 1024
        ),
    )(
        gated_input.reshape(steps, chans),
        query_gate.reshape(steps, chans),
        cotangent.reshape(steps, chans),
        skip_gain.reshape(1, chans),
        residues.T,
        decay_rates.T,
    )
    return output.reshape(gated_input.shape), update.T


def solution(mesh):
    sizes = tuple(mesh.shape[a] for a in ("seq", "batch", "chan"))
    return jax.shard_map(
        functools.partial(on_device, sizes),
        mesh=mesh,
        in_specs=(
            P("batch", "seq", "chan"),
            P("batch", "seq", "chan"),
            P("chan"),
            P("chan", None),
            P("chan", None),
            P("batch", "seq", "chan"),
        ),
        out_specs=(P("batch", "seq", "chan"), P("chan", None)),
        check_vma=False,
    )
```

```python
import functools

import jax
import jax.numpy as jnp
from jax import lax
from jax.experimental import pallas as pl
from jax.experimental.pallas import tpu as pltpu
from jax.sharding import PartitionSpec as P

MESH = pl.DeviceIdType.MESH
F32, BF16 = jnp.float32, jnp.bfloat16
HI = lax.Precision.HIGHEST
LANES = 128
CHUNKS = 4
NN = (((1,), (0,)), ((), ()))
NT = (((1,), (1,)), ((), ()))
TN = (((0,), (0,)), ((), ()))


def dot(a, b, dims=NN, precision=None):
    return lax.dot_general(a, b, dims, precision=precision, preferred_element_type=F32)


def iota(shape, dim):
    return lax.broadcasted_iota(jnp.int32, shape, dim)


def split(a):
    high = a.astype(BF16)
    return high, (a - high.astype(F32)).astype(BF16)


def split3(a):
    high, rest = a.astype(BF16), a
    rest = a - high.astype(F32)
    mid = rest.astype(BF16)
    return high, mid, (rest - mid.astype(F32)).astype(BF16)


def rows_by_one_hot(parts, one_hot):
    stacked = jnp.concatenate([p.astype(F32) for p in parts], axis=0).astype(BF16)
    return stacked, jnp.concatenate([one_hot] * len(parts), axis=0)


def kernel(
    sizes, width, modes,
    x_hbm, q_hbm, ct_hbm, skip_hbm, res_hbm, rate_hbm,
    out_ref, upd_ref,
    x_ref, q_ref, ct_ref, skip_ref, res_in, rate_in, res_ref, rate_ref, in_sem,
    s_ref, from_mate, dec_ref, filt_ref, q_sum, even_part, chain_in, chain_out,
    own_c, mate_c, other_c, near_ref, grad_in, sd_ref, fall_ref, g_ref, all_g, tot_ref,
    mate_sem, chain_sem, back_sem, g_send, g_recv, twin_sem,
):
    n_seq, n_batch, n_chan = sizes
    pairs = n_seq // 2
    steps, chans = x_hbm.shape
    tiles = chans // LANES
    half = tiles // 2
    per = LANES // width
    lane_of = iota((1, LANES), 1)
    seq, bat, cha = (lax.axis_index(a) for a in ("seq", "batch", "chan"))
    parity, line = lax.rem(seq, 2), lax.div(seq, 2)

    def dev(s, b=bat, c=cha):
        return {"seq": s, "batch": b, "chan": c}

    def fetch(n, src, dst):
        copy = pltpu.make_async_copy(src, dst, in_sem.at[n])
        copy.start()
        return copy

    def columns(h):
        return pl.ds(pl.multiple_of(h * (half * LANES), LANES), half * LANES)

    other = 1 - parity
    get_rate = fetch(0, rate_hbm, rate_in)
    get_res = fetch(1, res_hbm, res_in)
    get_x1 = fetch(2, x_hbm.at[:, columns(other)], x_ref.at[:, columns(other)])
    get_x2 = fetch(3, x_hbm.at[:, columns(parity)], x_ref.at[:, columns(parity)])
    get_q = fetch(4, q_hbm, q_ref)
    get_ct = fetch(5, ct_hbm, ct_ref)
    get_skip = fetch(6, skip_hbm, skip_ref)

    mate = dev(seq + 1 - 2 * parity)
    group_row = iota((LANES, LANES), 0) // width
    group_col = iota((LANES, LANES), 1) // width
    same = group_row == group_col
    lower = iota((steps, steps), 0) >= iota((steps, steps), 1)
    index_sum = iota((steps, steps), 0) + iota((steps, steps), 1)
    corner = index_sum <= steps - 1
    reverse = jnp.where(index_sum == steps - 1, 1.0, 0.0).astype(BF16)
    pick = (iota((per, LANES), 0) == iota((per, LANES), 1) // modes)

    barrier = pltpu.get_barrier_semaphore()

    def greet(d):
        pl.semaphore_signal(barrier, inc=1, device_id=d, device_id_type=MESH)

    members = n_seq * n_batch
    me = bat * n_seq + seq
    twin = dev(seq, bat, 1 - cha)

    def member(m):
        there = lax.rem(me + m, members)
        return there, dev(lax.rem(there, n_seq), lax.div(there, n_seq))

    def greet_member(m, _):
        greet(member(m)[1])
        return 0

    lax.fori_loop(1, members, greet_member, 0)
    greet(twin)
    count = members

    @pl.when(line > 0)
    def _():
        greet(dev(seq - 2))

    @pl.when(line < pairs - 1)
    def _():
        greet(dev(seq + 2))

    count = count + jnp.where(line > 0, 1, 0) + jnp.where(line < pairs - 1, 1, 0)

    back = (steps - 1 - iota((steps, LANES), 0)).astype(F32)
    select = (iota((modes, LANES), 1) % modes) == iota((modes, LANES), 0)
    one_hot = jnp.where(same, 1.0, 0.0).astype(BF16)

    def state_tile(h, j):
        i = h * half + j
        at = pl.ds(pl.multiple_of(i * LANES, LANES), LANES)
        lanes = pl.ds(pl.multiple_of(j * LANES, LANES), LANES)
        rate = rate_ref[pl.ds(i, 1), :]
        res = res_ref[pl.ds(i, 1), :]
        falling = jnp.exp(-rate * back)
        fall_ref[i] = falling
        f_hi, f_lo = split(falling)
        full = dot(f_hi, x_ref[:, at], TN)
        full = jnp.where(same, full, 0.0).reshape(per, modes, LANES)
        s_ref[h, :, lanes] = jnp.sum(full, axis=0)
        w_hi, w_lo = split(jnp.where(pick, res, 0.0))
        filt_ref[pl.ds(pl.multiple_of(i * per, per), per), :] = dot(
            jnp.concatenate([w_hi, w_hi, w_lo], axis=1),
            jnp.concatenate([f_hi, f_lo, f_hi], axis=1),
            NT,
        )
        decay = jnp.exp(-rate * float(steps))
        spread = dot(
            jnp.concatenate(split3(jnp.where(select, decay, 0.0)), axis=0), one_hot
        )
        dec_ref[h, :, lanes] = spread[:modes] + spread[modes : 2 * modes] + spread[2 * modes :]

    def other_two(j, _):
        state_tile(other, 2 * j)
        state_tile(other, 2 * j + 1)
        return 0

    def own_two(j, _):
        state_tile(parity, 2 * j)
        state_tile(parity, 2 * j + 1)
        return 0

    groups = tiles * per
    row_group = lax.rem(iota((groups, LANES), 0), per) == iota((groups, LANES), 1) // modes
    mode_hot = jnp.where(select, 1.0, 0.0).astype(BF16)

    def by_rows(ref):
        left, right = rows_by_one_hot(split3(ref[...]), mode_hot)
        wide = jnp.where(row_group, dot(left, right, TN), 0.0)
        return jnp.sum(wide.reshape(tiles, per, LANES), axis=1)

    get_rate.wait()
    rate_ref[...] = by_rows(rate_in)
    get_res.wait()
    res_ref[...] = by_rows(res_in)
    get_x1.wait()
    lax.fori_loop(0, half // 2, other_two, 0)
    pl.semaphore_wait(barrier, count)
    to_mate = pltpu.make_async_remote_copy(
        s_ref.at[other], from_mate, mate_sem.at[0], mate_sem.at[1], device_id=mate,
        device_id_type=MESH,
    )
    to_mate.start()
    get_x2.wait()
    lax.fori_loop(0, half // 2, own_two, 0)
    get_q.wait()
    get_ct.wait()
    get_skip.wait()

    part = half * LANES // CHUNKS

    def chain_copy(k):
        return pltpu.make_async_remote_copy(
            chain_out.at[k], chain_in.at[k], chain_sem.at[0, k], chain_sem.at[1, k],
            device_id=dev(jnp.minimum(seq + 2, n_seq - 1 - (1 - parity))), device_id_type=MESH,
        )

    def back_copy(k):
        return pltpu.make_async_remote_copy(
            mate_c.at[k], other_c.at[k], back_sem.at[0, k], back_sem.at[1, k], device_id=mate,
            device_id_type=MESH,
        )

    def chain_step():
        to_mate.wait_recv()
        for k in range(CHUNKS):
            cols = slice(k * part, (k + 1) * part)
            mine, his = s_ref[parity, :, cols], from_mate[:, cols]
            early = jnp.where(parity == 0, mine, his)
            late = jnp.where(parity == 0, his, mine)
            q_sum[:, cols] = dec_ref[parity, :, cols] * early + late
            even_part[:, cols] = early

        for k in range(CHUNKS):
            cols = slice(k * part, (k + 1) * part)
            decay = dec_ref[parity, :, cols]
            early = even_part[:, cols]

            def finish(carry):
                @pl.when(line < pairs - 1)
                def _():
                    chain_out[k] = decay * decay * carry + q_sum[:, cols]
                    chain_copy(k).start()

                after = decay * carry + early
                mate_c[k] = jnp.where(parity == 0, after, carry)
                back_copy(k).start()
                own_c[k] = jnp.where(parity == 0, carry, after)

            @pl.when(line == 0)
            def _():
                finish(jnp.zeros((modes, part), F32))

            @pl.when(line > 0)
            def _():
                chain_copy(k).wait_recv()
                finish(chain_in[k])

    trigger = jnp.minimum(1 + lax.div(line * half, pairs), half - 1)
    ahead = (iota((steps, LANES), 0) + 1).astype(F32)

    def near_tile(i):
        at = pl.ds(pl.multiple_of(i * LANES, LANES), LANES)
        x = x_ref[:, at]
        grad = (ct_ref[:, at].astype(F32) * q_ref[:, at].astype(F32)).astype(BF16)
        grad_in[:, at] = grad
        zero = jnp.zeros((), BF16)
        stacked = jnp.concatenate(
            [jnp.where(lane_of // width == g, x, zero) for g in range(per)], axis=0
        )
        filt = filt_ref[pl.ds(pl.multiple_of(i * per, per), per), :]
        filt = filt.astype(BF16).astype(F32)
        blocks = []
        for g in range(per):
            rows = jnp.broadcast_to(filt[g : g + 1, :], (steps, steps))
            rows = pltpu.roll(rows, 1, 1, stride=1, stride_axis=0)
            blocks.append(jnp.where(lower, rows, 0.0).astype(BF16))
        near = dot(jnp.concatenate(blocks, axis=1), stacked)
        near_ref[:, at] = near + skip_ref[:, at] * x.astype(F32)
        turned = dot(reverse, grad).astype(BF16)
        pair_sums = dot(stacked, turned, NT)
        totals = []
        for g in range(per):
            block = jnp.where(corner, pair_sums[g * steps : (g + 1) * steps], 0.0)
            block = pltpu.roll(block, 0, 1, stride=1, stride_axis=0)
            totals.append(jnp.sum(block, axis=0, keepdims=True))
        lag_sums = jnp.concatenate(totals, axis=0)
        rate = rate_ref[pl.ds(i, 1), :]
        start = jnp.exp(-rate * ahead)
        sd_ref[i] = start
        left, right = rows_by_one_hot(split3(lag_sums), jnp.where(pick, 1.0, 0.0))
        wide = dot(left, right.astype(BF16), TN)
        g_ref[pl.ds(i, 1), :] = jnp.sum(wide * fall_ref[i], axis=0, keepdims=True)

    def near_two(i, _):
        @pl.when(i == trigger)
        def _():
            chain_step()

        near_tile(2 * i)
        near_tile(2 * i + 1)
        return 0

    lax.fori_loop(0, half, near_two, 0)

    per_chunk = half // CHUNKS

    def far_tile(h, k, j, carried_ref):
        i = h * half + k * per_chunk + j
        at = pl.ds(pl.multiple_of(i * LANES, LANES), LANES)
        lanes = pl.ds(pl.multiple_of(j * LANES, LANES), LANES)
        carried = carried_ref[k, :, lanes]
        carried = jnp.broadcast_to(carried[None], (per, modes, LANES)).reshape(LANES, LANES)
        c_hi, c_lo = split(jnp.where(same, carried, 0.0))
        start = sd_ref[i]
        a_hi, a_lo = split(res_ref[pl.ds(i, 1), :] * start)
        far = dot(
            jnp.concatenate([a_hi, a_hi, a_lo], axis=1),
            jnp.concatenate([c_hi, c_lo, c_hi], axis=0),
        )
        gate = q_ref[:, at].astype(F32)
        out_ref[:, at] = (gate * (near_ref[:, at] + far)).astype(BF16)
        grad = grad_in[:, at]
        mixed = dot(grad, c_hi, NT) + dot(grad, c_lo, NT)
        gain = jnp.sum(mixed * start.astype(BF16).astype(F32), axis=0, keepdims=True)
        g_ref[pl.ds(i, 1), :] += gain

    def far_loop(h, k, carried_ref):
        def body(j, _):
            far_tile(h, k, 2 * j, carried_ref)
            far_tile(h, k, 2 * j + 1, carried_ref)
            return 0

        lax.fori_loop(0, max(1, per_chunk // 2), body, 0)

    for k in range(CHUNKS):
        far_loop(parity, k, own_c)
    for k in range(CHUNKS):
        back_copy(k).wait_recv()
        far_loop(other, k, other_c)

    def share(there, device, slot):
        return pltpu.make_async_remote_copy(
            g_ref, all_g.at[slot], g_send.at[there], g_recv.at[slot],
            device_id=device, device_id_type=MESH,
        )

    def send_member(m, _):
        there, device = member(m)
        share(there, device, me).start()
        return 0

    def take_member(m, _):
        there, device = member(m)
        share(there, device, there).wait_recv()
        return 0

    lax.fori_loop(1, members, send_member, 0)
    all_g[me] = g_ref[...]
    lax.fori_loop(1, members, take_member, 0)
    tot_ref[0] = jnp.sum(all_g[...], axis=0)
    to_twin = pltpu.make_async_remote_copy(
        tot_ref.at[0], tot_ref.at[1], twin_sem.at[0], twin_sem.at[1], device_id=twin,
        device_id_type=MESH,
    )
    to_twin.start()
    to_twin.wait_recv()
    square = jnp.sum(tot_ref[...] * tot_ref[...], keepdims=True).reshape(1, 1)
    limit = jnp.sqrt(jnp.float32(tiles * LANES * n_chan))
    scale = jnp.minimum(1.0, limit / jnp.sqrt(square + 1e-06))
    rows = tot_ref[0] * scale
    rows = jnp.broadcast_to(rows[:, None, :], (tiles, per, LANES)).reshape(groups, LANES)
    rows = jnp.concatenate(split3(jnp.where(row_group, rows, 0.0)), axis=1)
    upd_ref[...] = dot(jnp.concatenate([mode_hot] * 3, axis=1), rows, NT)

    def sent_member(m, _):
        there, device = member(m)
        share(there, device, me).wait_send()
        return 0

    lax.fori_loop(1, members, sent_member, 0)
    to_twin.wait_send()
    to_mate.wait_send()
    for k in range(CHUNKS):
        back_copy(k).wait_send()

        @pl.when(line < pairs - 1)
        def _():
            chain_copy(k).wait_send()


def on_device(sizes, gated_input, query_gate, skip_gain, residues, decay_rates, cotangent):
    _, steps, chans = gated_input.shape
    groups, modes = residues.shape
    width = chans // groups
    tiles = chans // LANES
    half = tiles // 2
    pairs = sizes[0] // 2
    members = sizes[0] * sizes[1]
    part = half * LANES // CHUNKS
    wide = half * LANES
    vmem = pl.BlockSpec(memory_space=pltpu.VMEM)
    dma = pltpu.SemaphoreType.DMA
    output, update = pl.pallas_call(
        functools.partial(kernel, sizes, width, modes),
        out_shape=(
            jax.ShapeDtypeStruct((steps, chans), BF16),
            jax.ShapeDtypeStruct((modes, groups), F32),
        ),
        in_specs=[pl.BlockSpec(memory_space=pltpu.HBM)] * 6,
        out_specs=(vmem, vmem),
        scratch_shapes=[
            pltpu.VMEM((steps, chans), BF16),
            pltpu.VMEM((steps, chans), BF16),
            pltpu.VMEM((steps, chans), BF16),
            pltpu.VMEM((1, chans), F32),
            pltpu.VMEM((modes, groups), F32),
            pltpu.VMEM((modes, groups), F32),
            pltpu.VMEM((tiles, LANES), F32),
            pltpu.VMEM((tiles, LANES), F32),
            dma((7,)),
            pltpu.VMEM((2, modes, wide), F32),
            pltpu.VMEM((modes, wide), F32),
            pltpu.VMEM((2, modes, wide), F32),
            pltpu.VMEM((groups, steps), F32),
            pltpu.VMEM((modes, wide), F32),
            pltpu.VMEM((modes, wide), F32),
            pltpu.VMEM((CHUNKS, modes, part), F32),
            pltpu.VMEM((CHUNKS, modes, part), F32),
            pltpu.VMEM((CHUNKS, modes, part), F32),
            pltpu.VMEM((CHUNKS, modes, part), F32),
            pltpu.VMEM((CHUNKS, modes, part), F32),
            pltpu.VMEM((steps, chans), F32),
            pltpu.VMEM((steps, chans), BF16),
            pltpu.VMEM((tiles, steps, LANES), F32),
            pltpu.VMEM((tiles, steps, LANES), F32),
            pltpu.VMEM((tiles, LANES), F32),
            pltpu.VMEM((members, tiles, LANES), F32),
            pltpu.VMEM((2, tiles, LANES), F32),
            dma((2,)),
            dma((2, CHUNKS)),
            dma((2, CHUNKS)),
            dma((members,)),
            dma((members,)),
            dma((2,)),
        ],
        compiler_params=pltpu.CompilerParams(
            collective_id=0, has_side_effects=True, vmem_limit_bytes=60 * 1024 * 1024
        ),
    )(
        gated_input.reshape(steps, chans),
        query_gate.reshape(steps, chans),
        cotangent.reshape(steps, chans),
        skip_gain.reshape(1, chans),
        residues.T,
        decay_rates.T,
    )
    return output.reshape(gated_input.shape), update.T


def solution(mesh):
    sizes = tuple(mesh.shape[a] for a in ("seq", "batch", "chan"))
    return jax.shard_map(
        functools.partial(on_device, sizes),
        mesh=mesh,
        in_specs=(
            P("batch", "seq", "chan"),
            P("batch", "seq", "chan"),
            P("chan"),
            P("chan", None),
            P("chan", None),
            P("batch", "seq", "chan"),
        ),
        out_specs=(P("batch", "seq", "chan"), P("chan", None)),
        check_vma=False,
    )
```

```python
import functools

import jax
import jax.numpy as jnp
from jax import lax
from jax.experimental import pallas as pl
from jax.experimental.pallas import tpu as pltpu
from jax.sharding import PartitionSpec as P

MESH = pl.DeviceIdType.MESH
F32, BF16 = jnp.float32, jnp.bfloat16
HI = lax.Precision.HIGHEST
LANES = 128
CHUNKS = 4
NN = (((1,), (0,)), ((), ()))
NT = (((1,), (1,)), ((), ()))
TN = (((0,), (0,)), ((), ()))


def dot(a, b, dims=NN, precision=None):
    return lax.dot_general(a, b, dims, precision=precision, preferred_element_type=F32)


def iota(shape, dim):
    return lax.broadcasted_iota(jnp.int32, shape, dim)


def split(a):
    high = a.astype(BF16)
    return high, (a - high.astype(F32)).astype(BF16)


def split3(a):
    high, rest = a.astype(BF16), a
    rest = a - high.astype(F32)
    mid = rest.astype(BF16)
    return high, mid, (rest - mid.astype(F32)).astype(BF16)


def rows_by_one_hot(parts, one_hot):
    stacked = jnp.concatenate([p.astype(F32) for p in parts], axis=0).astype(BF16)
    return stacked, jnp.concatenate([one_hot] * len(parts), axis=0)


def kernel(
    sizes, width, modes,
    x_hbm, q_hbm, ct_hbm, skip_hbm, res_hbm, rate_hbm,
    out_ref, upd_ref,
    x_ref, q_ref, ct_ref, skip_ref, res_in, rate_in, res_ref, rate_ref, in_sem,
    s_ref, from_mate, dec_ref, filt_ref, q_sum, even_part, chain_in,
    own_c, mate_c, other_c, near_ref, grad_in, sd_ref, fall_ref, g_ref, all_g, tot_ref,
    mate_sem, chain_sem, back_sem, g_send, g_recv, twin_sem,
):
    n_seq, n_batch, n_chan = sizes
    pairs = n_seq // 2
    steps, chans = x_hbm.shape
    tiles = chans // LANES
    half = tiles // 2
    per = LANES // width
    lane_of = iota((1, LANES), 1)
    seq, bat, cha = (lax.axis_index(a) for a in ("seq", "batch", "chan"))
    parity, line = lax.rem(seq, 2), lax.div(seq, 2)

    def dev(s, b=bat, c=cha):
        return {"seq": s, "batch": b, "chan": c}

    def fetch(n, src, dst):
        copy = pltpu.make_async_copy(src, dst, in_sem.at[n])
        copy.start()
        return copy

    def columns(h):
        return pl.ds(pl.multiple_of(h * (half * LANES), LANES), half * LANES)

    other = 1 - parity
    get_rate = fetch(0, rate_hbm, rate_in)
    get_res = fetch(1, res_hbm, res_in)
    get_x1 = fetch(2, x_hbm.at[:, columns(other)], x_ref.at[:, columns(other)])
    get_x2 = fetch(3, x_hbm.at[:, columns(parity)], x_ref.at[:, columns(parity)])
    get_q = fetch(4, q_hbm, q_ref)
    get_ct = fetch(5, ct_hbm, ct_ref)
    get_skip = fetch(6, skip_hbm, skip_ref)

    mate = dev(seq + 1 - 2 * parity)
    group_row = iota((LANES, LANES), 0) // width
    group_col = iota((LANES, LANES), 1) // width
    same = group_row == group_col
    lower = iota((steps, steps), 0) >= iota((steps, steps), 1)
    index_sum = iota((steps, steps), 0) + iota((steps, steps), 1)
    corner = index_sum <= steps - 1
    reverse = jnp.where(index_sum == steps - 1, 1.0, 0.0).astype(BF16)
    pick = (iota((per, LANES), 0) == iota((per, LANES), 1) // modes)

    barrier = pltpu.get_barrier_semaphore()

    def greet(d):
        pl.semaphore_signal(barrier, inc=1, device_id=d, device_id_type=MESH)

    members = n_seq * n_batch
    me = bat * n_seq + seq
    twin = dev(seq, bat, 1 - cha)

    def member(m):
        there = lax.rem(me + m, members)
        return there, dev(lax.rem(there, n_seq), lax.div(there, n_seq))

    def greet_member(m, _):
        greet(member(m)[1])
        return 0

    lax.fori_loop(1, members, greet_member, 0)
    greet(twin)
    count = members

    @pl.when(line > 0)
    def _():
        greet(dev(seq - 2))

    @pl.when(line < pairs - 1)
    def _():
        greet(dev(seq + 2))

    count = count + jnp.where(line > 0, 1, 0) + jnp.where(line < pairs - 1, 1, 0)

    back = (steps - 1 - iota((steps, LANES), 0)).astype(F32)
    select = (iota((modes, LANES), 1) % modes) == iota((modes, LANES), 0)
    one_hot = jnp.where(same, 1.0, 0.0).astype(BF16)

    def state_tile(h, j):
        i = h * half + j
        at = pl.ds(pl.multiple_of(i * LANES, LANES), LANES)
        lanes = pl.ds(pl.multiple_of(j * LANES, LANES), LANES)
        rate = rate_ref[pl.ds(i, 1), :]
        res = res_ref[pl.ds(i, 1), :]
        falling = jnp.exp(-rate * back)
        fall_ref[i] = falling
        f_hi, f_lo = split(falling)
        full = dot(f_hi, x_ref[:, at], TN)
        full = jnp.where(same, full, 0.0).reshape(per, modes, LANES)
        s_ref[h, :, lanes] = jnp.sum(full, axis=0)
        w_hi, w_lo = split(jnp.where(pick, res, 0.0))
        filt_ref[pl.ds(pl.multiple_of(i * per, per), per), :] = dot(
            jnp.concatenate([w_hi, w_hi, w_lo], axis=1),
            jnp.concatenate([f_hi, f_lo, f_hi], axis=1),
            NT,
        )
        decay = jnp.exp(-rate * float(steps))
        spread = dot(
            jnp.concatenate(split3(jnp.where(select, decay, 0.0)), axis=0), one_hot
        )
        dec_ref[h, :, lanes] = spread[:modes] + spread[modes : 2 * modes] + spread[2 * modes :]

    def other_two(j, _):
        state_tile(other, 2 * j)
        state_tile(other, 2 * j + 1)
        return 0

    def own_two(j, _):
        state_tile(parity, 2 * j)
        state_tile(parity, 2 * j + 1)
        return 0

    groups = tiles * per
    row_group = lax.rem(iota((groups, LANES), 0), per) == iota((groups, LANES), 1) // modes
    mode_hot = jnp.where(select, 1.0, 0.0).astype(BF16)

    def by_rows(ref):
        left, right = rows_by_one_hot(split3(ref[...]), mode_hot)
        wide = jnp.where(row_group, dot(left, right, TN), 0.0)
        return jnp.sum(wide.reshape(tiles, per, LANES), axis=1)

    get_rate.wait()
    rate_ref[...] = by_rows(rate_in)
    get_res.wait()
    res_ref[...] = by_rows(res_in)
    get_x1.wait()
    lax.fori_loop(0, half // 2, other_two, 0)
    pl.semaphore_wait(barrier, count)
    to_mate = pltpu.make_async_remote_copy(
        s_ref.at[other], from_mate, mate_sem.at[0], mate_sem.at[1], device_id=mate,
        device_id_type=MESH,
    )
    to_mate.start()
    get_x2.wait()
    lax.fori_loop(0, half // 2, own_two, 0)
    get_q.wait()
    get_ct.wait()
    get_skip.wait()

    part = half * LANES // CHUNKS

    def line_copy(slot, there):
        return pltpu.make_async_remote_copy(
            q_sum, chain_in.at[slot], chain_sem.at[0, there], chain_sem.at[1, slot],
            device_id=dev(2 * there + parity), device_id_type=MESH,
        )

    def back_copy(k):
        return pltpu.make_async_remote_copy(
            mate_c.at[k], other_c.at[k], back_sem.at[0, k], back_sem.at[1, k], device_id=mate,
            device_id_type=MESH,
        )

    def send_step():
        to_mate.wait_recv()
        for k in range(CHUNKS):
            cols = slice(k * part, (k + 1) * part)
            mine, his = s_ref[parity, :, cols], from_mate[:, cols]
            early = jnp.where(parity == 0, mine, his)
            late = jnp.where(parity == 0, his, mine)
            q_sum[:, cols] = dec_ref[parity, :, cols] * early + late
            even_part[:, cols] = early

        def send_line(there, _):
            line_copy(line, there).start()
            return 0

        lax.fori_loop(line + 1, pairs, send_line, 0)

    def carry_step():
        decay = dec_ref[parity]
        twice = decay * decay

        def take_line(slot, carry):
            line_copy(slot, slot).wait_recv()
            return twice * carry + chain_in[slot]

        carry = lax.fori_loop(0, line, take_line, jnp.zeros((modes, half * LANES), F32))
        after = decay * carry + even_part[...]
        mine = jnp.where(parity == 0, carry, after)
        his = jnp.where(parity == 0, after, carry)
        for k in range(CHUNKS):
            cols = slice(k * part, (k + 1) * part)
            mate_c[k] = his[:, cols]
            back_copy(k).start()
            own_c[k] = mine[:, cols]

    send_at, carry_at = min(1, half - 1), max(1, half - 2)
    ahead = (iota((steps, LANES), 0) + 1).astype(F32)

    def near_tile(i):
        at = pl.ds(pl.multiple_of(i * LANES, LANES), LANES)
        x = x_ref[:, at]
        grad = (ct_ref[:, at].astype(F32) * q_ref[:, at].astype(F32)).astype(BF16)
        grad_in[:, at] = grad
        zero = jnp.zeros((), BF16)
        stacked = jnp.concatenate(
            [jnp.where(lane_of // width == g, x, zero) for g in range(per)], axis=0
        )
        filt = filt_ref[pl.ds(pl.multiple_of(i * per, per), per), :]
        filt = filt.astype(BF16).astype(F32)
        blocks = []
        for g in range(per):
            rows = jnp.broadcast_to(filt[g : g + 1, :], (steps, steps))
            rows = pltpu.roll(rows, 1, 1, stride=1, stride_axis=0)
            blocks.append(jnp.where(lower, rows, 0.0).astype(BF16))
        near = dot(jnp.concatenate(blocks, axis=1), stacked)
        near_ref[:, at] = near + skip_ref[:, at] * x.astype(F32)
        turned = dot(reverse, grad).astype(BF16)
        pair_sums = dot(stacked, turned, NT)
        totals = []
        for g in range(per):
            block = jnp.where(corner, pair_sums[g * steps : (g + 1) * steps], 0.0)
            block = pltpu.roll(block, 0, 1, stride=1, stride_axis=0)
            totals.append(jnp.sum(block, axis=0, keepdims=True))
        lag_sums = jnp.concatenate(totals, axis=0)
        rate = rate_ref[pl.ds(i, 1), :]
        start = jnp.exp(-rate * ahead)
        sd_ref[i] = start
        left, right = rows_by_one_hot(split3(lag_sums), jnp.where(pick, 1.0, 0.0))
        wide = dot(left, right.astype(BF16), TN)
        g_ref[pl.ds(i, 1), :] = jnp.sum(wide * fall_ref[i], axis=0, keepdims=True)

    def near_two(i, _):
        @pl.when(i == send_at)
        def _():
            send_step()

        @pl.when(i == carry_at)
        def _():
            carry_step()

        near_tile(2 * i)
        near_tile(2 * i + 1)
        return 0

    lax.fori_loop(0, half, near_two, 0)

    per_chunk = half // CHUNKS

    def far_tile(h, k, j, carried_ref):
        i = h * half + k * per_chunk + j
        at = pl.ds(pl.multiple_of(i * LANES, LANES), LANES)
        lanes = pl.ds(pl.multiple_of(j * LANES, LANES), LANES)
        carried = carried_ref[k, :, lanes]
        carried = jnp.broadcast_to(carried[None], (per, modes, LANES)).reshape(LANES, LANES)
        c_hi, c_lo = split(jnp.where(same, carried, 0.0))
        start = sd_ref[i]
        a_hi, a_lo = split(res_ref[pl.ds(i, 1), :] * start)
        far = dot(
            jnp.concatenate([a_hi, a_hi, a_lo], axis=1),
            jnp.concatenate([c_hi, c_lo, c_hi], axis=0),
        )
        gate = q_ref[:, at].astype(F32)
        out_ref[:, at] = (gate * (near_ref[:, at] + far)).astype(BF16)
        grad = grad_in[:, at]
        mixed = dot(grad, c_hi, NT) + dot(grad, c_lo, NT)
        gain = jnp.sum(mixed * start.astype(BF16).astype(F32), axis=0, keepdims=True)
        g_ref[pl.ds(i, 1), :] += gain

    def far_loop(h, k, carried_ref):
        def body(j, _):
            far_tile(h, k, 2 * j, carried_ref)
            far_tile(h, k, 2 * j + 1, carried_ref)
            return 0

        lax.fori_loop(0, max(1, per_chunk // 2), body, 0)

    for k in range(CHUNKS):
        far_loop(parity, k, own_c)
    for k in range(CHUNKS):
        back_copy(k).wait_recv()
        far_loop(other, k, other_c)

    def share(there, device, slot):
        return pltpu.make_async_remote_copy(
            g_ref, all_g.at[slot], g_send.at[there], g_recv.at[slot],
            device_id=device, device_id_type=MESH,
        )

    def send_member(m, _):
        there, device = member(m)
        share(there, device, me).start()
        return 0

    def take_member(m, _):
        there, device = member(m)
        share(there, device, there).wait_recv()
        return 0

    lax.fori_loop(1, members, send_member, 0)
    all_g[me] = g_ref[...]
    lax.fori_loop(1, members, take_member, 0)
    tot_ref[0] = jnp.sum(all_g[...], axis=0)
    to_twin = pltpu.make_async_remote_copy(
        tot_ref.at[0], tot_ref.at[1], twin_sem.at[0], twin_sem.at[1], device_id=twin,
        device_id_type=MESH,
    )
    to_twin.start()
    to_twin.wait_recv()
    square = jnp.sum(tot_ref[...] * tot_ref[...], keepdims=True).reshape(1, 1)
    limit = jnp.sqrt(jnp.float32(tiles * LANES * n_chan))
    scale = jnp.minimum(1.0, limit / jnp.sqrt(square + 1e-06))
    rows = tot_ref[0] * scale
    rows = jnp.broadcast_to(rows[:, None, :], (tiles, per, LANES)).reshape(groups, LANES)
    rows = jnp.concatenate(split3(jnp.where(row_group, rows, 0.0)), axis=1)
    upd_ref[...] = dot(jnp.concatenate([mode_hot] * 3, axis=1), rows, NT)

    def sent_member(m, _):
        there, device = member(m)
        share(there, device, me).wait_send()
        return 0

    lax.fori_loop(1, members, sent_member, 0)
    to_twin.wait_send()
    to_mate.wait_send()
    for k in range(CHUNKS):
        back_copy(k).wait_send()

    def sent_line(there, _):
        line_copy(line, there).wait_send()
        return 0

    lax.fori_loop(line + 1, pairs, sent_line, 0)


def on_device(sizes, gated_input, query_gate, skip_gain, residues, decay_rates, cotangent):
    _, steps, chans = gated_input.shape
    groups, modes = residues.shape
    width = chans // groups
    tiles = chans // LANES
    half = tiles // 2
    pairs = sizes[0] // 2
    members = sizes[0] * sizes[1]
    part = half * LANES // CHUNKS
    wide = half * LANES
    vmem = pl.BlockSpec(memory_space=pltpu.VMEM)
    dma = pltpu.SemaphoreType.DMA
    output, update = pl.pallas_call(
        functools.partial(kernel, sizes, width, modes),
        out_shape=(
            jax.ShapeDtypeStruct((steps, chans), BF16),
            jax.ShapeDtypeStruct((modes, groups), F32),
        ),
        in_specs=[pl.BlockSpec(memory_space=pltpu.HBM)] * 6,
        out_specs=(vmem, vmem),
        scratch_shapes=[
            pltpu.VMEM((steps, chans), BF16),
            pltpu.VMEM((steps, chans), BF16),
            pltpu.VMEM((steps, chans), BF16),
            pltpu.VMEM((1, chans), F32),
            pltpu.VMEM((modes, groups), F32),
            pltpu.VMEM((modes, groups), F32),
            pltpu.VMEM((tiles, LANES), F32),
            pltpu.VMEM((tiles, LANES), F32),
            dma((7,)),
            pltpu.VMEM((2, modes, wide), F32),
            pltpu.VMEM((modes, wide), F32),
            pltpu.VMEM((2, modes, wide), F32),
            pltpu.VMEM((groups, steps), F32),
            pltpu.VMEM((modes, wide), F32),
            pltpu.VMEM((modes, wide), F32),
            pltpu.VMEM((pairs, modes, wide), F32),
            pltpu.VMEM((CHUNKS, modes, part), F32),
            pltpu.VMEM((CHUNKS, modes, part), F32),
            pltpu.VMEM((CHUNKS, modes, part), F32),
            pltpu.VMEM((steps, chans), F32),
            pltpu.VMEM((steps, chans), BF16),
            pltpu.VMEM((tiles, steps, LANES), F32),
            pltpu.VMEM((tiles, steps, LANES), F32),
            pltpu.VMEM((tiles, LANES), F32),
            pltpu.VMEM((members, tiles, LANES), F32),
            pltpu.VMEM((2, tiles, LANES), F32),
            dma((2,)),
            dma((2, pairs)),
            dma((2, CHUNKS)),
            dma((members,)),
            dma((members,)),
            dma((2,)),
        ],
        compiler_params=pltpu.CompilerParams(
            collective_id=0, has_side_effects=True, vmem_limit_bytes=60 * 1024 * 1024
        ),
    )(
        gated_input.reshape(steps, chans),
        query_gate.reshape(steps, chans),
        cotangent.reshape(steps, chans),
        skip_gain.reshape(1, chans),
        residues.T,
        decay_rates.T,
    )
    return output.reshape(gated_input.shape), update.T


def solution(mesh):
    sizes = tuple(mesh.shape[a] for a in ("seq", "batch", "chan"))
    return jax.shard_map(
        functools.partial(on_device, sizes),
        mesh=mesh,
        in_specs=(
            P("batch", "seq", "chan"),
            P("batch", "seq", "chan"),
            P("chan"),
            P("chan", None),
            P("chan", None),
            P("batch", "seq", "chan"),
        ),
        out_specs=(P("batch", "seq", "chan"), P("chan", None)),
        check_vma=False,
    )
```
